32 devices in a mesh: dp: 4 (over x, core), mp: 8 (over z, y).
Axes of the slice: x: 2, y: 2, z: 4, core: 2. Of those that a mesh axis runs over, the one named last changes fastest.
Arguments:
- fields: float32 [4, 32, 128, 128, 128], P('dp', None, 'mp'), may hold values from -6 to 6
- upstream: bfloat16 [4, 32, 128, 128, 128], P('dp', None, 'mp'), may hold values from -6 to 6
- spectral_weight: float32 [2, 32, 32, 32, 1024], P(None, None, None, 'dp', 'mp'), may hold values from -4.2 to 4.2
- point_weight: float32 [32, 32], replicated, may hold values from -1 to 1
- point_bias: float32 [32], replicated, may hold values from -3 to 3
Outputs:
- grad_fields: float32 [4, 32, 128, 128, 128], P('dp', None, 'mp')
- grad_weight: float32 [2, 32, 32, 32, 1024], P(None, None, None, 'dp', 'mp')
The draws below stay inside these ranges and needn't reach their ends.
All inputs are finite; a program needn't handle non-finite values.
Results may differ from the reference program's by a relative error of at most 0.0003.
Values sent between devices are 32-bit elements; how exact they have to be, the bound alone decides.
No kernel may reach another device: no remote copies, remote signals or barrier semaphores. Data moves between devices by JAX's collectives and lax.ppermute only.
A program may use at most 320 MiB of HBM per device.

```python
import jax
import jax.numpy as jnp
from jax import lax

C = 32
NX = 128
NY = 128
NZ = 128
MX = 32
MY = 32
MZ = 32
BATCH = 4
MYZ = 1024


def block_levels(rng, extent, pieces, low, largest):
    loudness, own = 1.0, jax.random.fold_in(rng, 6)
    for axis_at, parts in pieces:
        draws = jnp.exp(jax.random.uniform(jax.random.fold_in(own, axis_at), (parts,), jnp.float32, low / len(pieces), largest / len(pieces)))
        loudness = loudness * jnp.repeat(draws, extent[axis_at] // parts).reshape([-1 if axis == axis_at else 1 for axis in range(len(extent))])
    return loudness


def normal_values(stream_key, dims, deviation, limit, split=(), held_as=jnp.bfloat16):
    factor_of = block_levels(stream_key, dims, split, -0.22, 0.18) if split else 1.0
    entries = jax.random.normal(stream_key, dims, jnp.float32) * deviation * factor_of
    return jnp.minimum(jnp.maximum(entries, -limit), limit).astype(held_as)


def setup_inputs(seed: int = 0) -> dict:
    splits = jax.random.split(jax.random.key(seed), 6)
    return {
        "fields": normal_values(splits[0], (BATCH, C, NX, NY, NZ), 1.0, 6.0, ((0, 4), (2, 8)), jnp.float32),
        "upstream": normal_values(splits[1], (BATCH, C, NX, NY, NZ), 1.0, 6.0, ((0, 4), (2, 8))),
        "spectral_weight": normal_values(splits[2], (2, C, C, MX, MYZ), 0.7, 4.2, ((3, 4), (4, 8)), jnp.float32),
        "point_weight": normal_values(splits[3], (C, C), C ** -0.5, 1.0, (), jnp.float32),
        "point_bias": normal_values(splits[4], (C,), 0.5, 3.0, (), jnp.float32),
    }


HIGHEST = lax.Precision.HIGHEST

def spectral(grid_field, weight):
    half_x = MX // 2
    half_y = MY // 2
    full_spec = jnp.fft.rfftn(grid_field, axes=(1, 2, 3))
    x_rows = jnp.concatenate([full_spec[:, :half_x], full_spec[:, NX - half_x:]], axis=1)
    kept_spec = jnp.concatenate([x_rows[:, :, :half_y], x_rows[:, :, NY - half_y:]], axis=2)[:, :, :, :MZ]
    coeffs = lax.complex(weight[0], weight[1]).reshape(C, C, MX, MY, MZ)
    mixed_spec = jnp.einsum('ixyz,ioxyz->oxyz', kept_spec, coeffs, precision=HIGHEST)
    padded = jnp.zeros((C, NX, NY, NZ // 2 + 1), mixed_spec.dtype)
    padded = padded.at[:, :half_x, :half_y, :MZ].set(mixed_spec[:, :half_x, :half_y])
    padded = padded.at[:, NX - half_x:, :half_y, :MZ].set(mixed_spec[:, half_x:, :half_y])
    padded = padded.at[:, :half_x, NY - half_y:, :MZ].set(mixed_spec[:, :half_x, half_y:])
    padded = padded.at[:, NX - half_x:, NY - half_y:, :MZ].set(mixed_spec[:, half_x:, half_y:])
    return jnp.fft.irfftn(padded, s=(NX, NY, NZ), axes=(1, 2, 3))

def reference(fields, upstream, spectral_weight, point_weight, point_bias):

    def layer_map(grid_field, weight):
        preact = spectral(grid_field, weight)
        preact = preact + jnp.einsum('cxyz,co->oxyz', grid_field, point_weight, precision=HIGHEST)
        preact = preact + point_bias[:, None, None, None]
        return jax.nn.gelu(preact, approximate=False)

    def sample_step(running, inputs_pair):
        grid_field, cotangent = inputs_pair
        activation, pullback = jax.vjp(layer_map, grid_field, spectral_weight)
        grad_field, grad_part = pullback(cotangent.astype(grid_field.dtype))
        return (running + grad_part, grad_field)
    running, grads = lax.scan(sample_step, jnp.zeros_like(spectral_weight), (fields, upstream))
    return (grads, running)
```

```python
from functools import partial
import math

import jax
import jax.numpy as jnp
import ml_dtypes
import numpy as np
from jax import lax
from jax.experimental import pallas as pl
from jax.experimental.pallas import tpu as pltpu
from jax.sharding import PartitionSpec as P

NX = 128
NY = 128
NZ = 128
MX = 32
MY = 32
MZ = 32
CELLS = NX * NY * NZ
HI = 8
LO = MY // HI
LANES = LO * MZ
CHUNKS = 2
PARTS = 4
F32 = jnp.float32
BF16 = jnp.bfloat16
VMEM_BYTES = 56 * 1024 * 1024


def signed(j, kept):
    return np.where(j < kept // 2, j, j - kept)


def second_order(slabs, half):
    parts = slabs // HI
    each = LO // parts
    at = np.arange(MY).reshape(HI, LO)
    place = (at // LO) * parts + (at % LO) // each
    slab = ((place % 2) ^ half) * (slabs // 2) + place // 2
    return slab * each + at % each


def waves(number, frequencies):
    phases = np.mod(np.arange(number)[:, None] * frequencies[None, :], number) * (2.0 * np.pi / number)
    return np.cos(phases), np.sin(phases)


def two_parts(table):
    high = table.astype(ml_dtypes.bfloat16)
    low = (table - high.astype(np.float64)).astype(ml_dtypes.bfloat16)
    return high, low


def stack_left(table):
    high, low = two_parts(table)
    return np.concatenate([high, high, low], axis=1)


def stack_right(table):
    high, low = two_parts(table)
    return np.concatenate([high, high, low], axis=0)


def y_forward(slabs, half):
    cos, sin = waves(NY, signed(np.arange(MY), MY))
    order = second_order(slabs, half)
    rows = np.stack([cos[:, order], sin[:, order]], axis=0)
    table = rows.transpose(3, 0, 2, 1).reshape(LO * 2 * HI, NY)
    high, low = two_parts(table)
    top = np.concatenate([high, high], axis=1)
    bottom = np.concatenate([low, np.zeros_like(low)], axis=1)
    return np.concatenate([top, bottom], axis=0)


def y_inverse(slabs, half):
    cos, sin = waves(NY, signed(np.arange(MY), MY))
    order = second_order(slabs, half)
    rows = np.stack([cos[:, order], -sin[:, order]], axis=0)
    return stack_left(rows.transpose(1, 3, 0, 2).reshape(NY, LO * 2 * HI))


def mode_factor():
    return np.where(np.arange(MZ) == 0, 1.0, 2.0) / CELLS


def z_forward(scaled):
    cos, sin = waves(NZ, np.arange(MZ))
    scale = mode_factor() if scaled else np.ones(MZ)
    small = np.zeros((2, NZ, 2, MZ))
    small[0, :, 0] = cos * scale
    small[1, :, 0] = -sin * scale
    small[0, :, 1] = -sin * scale
    small[1, :, 1] = -cos * scale
    table = np.zeros((LO, 2, NZ, 2, LO, MZ))
    for a in range(LO):
        table[a, :, :, :, a, :] = small
    return stack_right(table.reshape(LO * 2 * NZ, 2 * LANES))


def z_inverse(scaled):
    cos, sin = waves(NZ, np.arange(MZ))
    scale = mode_factor() if scaled else np.ones(MZ)
    small = np.zeros((2, MZ, 2, NZ))
    small[0, :, 0] = (cos * scale).T
    small[1, :, 0] = (-sin * scale).T
    small[0, :, 1] = (sin * scale).T
    small[1, :, 1] = (cos * scale).T
    table = np.zeros((2, LO, MZ, LO, 2, NZ))
    for a in range(LO):
        table[:, a, :, a, :, :] = small
    return stack_right(table.reshape(2 * LANES, LO * 2 * NZ))


def x_table(groups, slabs, half, group):
    cos, sin = waves(NX, signed(np.arange(MX), MX))
    near = slabs // 2
    cells = NX // slabs
    order = np.arange(MX).reshape(groups, MX // groups)[np.arange(groups) ^ group]
    rows = slice(half * (NX // 2), (half + 1) * (NX // 2))
    return [t[rows][:, order].reshape(near, cells, groups, MX // groups) for t in (cos, sin)]


def x_forward(groups, slabs, half, group):
    cos, sin = [t.transpose(2, 3, 0, 1) for t in x_table(groups, slabs, half, group)]
    table = np.zeros((groups, 2, MX // groups, slabs // 2, 2, NX // slabs))
    table[:, 0, :, :, 0] = cos
    table[:, 0, :, :, 1] = sin
    table[:, 1, :, :, 0] = -sin
    table[:, 1, :, :, 1] = cos
    return stack_left(table.reshape(2 * MX, NX))


def x_inverse(groups, slabs, half, group):
    cos, sin = [t.transpose(0, 1, 2, 3) for t in x_table(groups, slabs, half, group)]
    table = np.zeros((slabs // 2, 2, NX // slabs, groups, 2, MX // groups))
    table[:, 0, :, :, 0] = cos
    table[:, 0, :, :, 1] = -sin
    table[:, 1, :, :, 0] = sin
    table[:, 1, :, :, 1] = cos
    return stack_left(table.reshape(NX, 2 * MX))


def split(values):
    high = values.astype(BF16)
    return high, (values - high.astype(F32)).astype(BF16)


def dot(left, right):
    return jnp.dot(left, right, preferred_element_type=F32)


def rows3(values):
    high, low = split(values)
    return jnp.concatenate([high, low, high], axis=0)


def lanes3(values):
    high, low = split(values)
    return jnp.concatenate([high, low, high], axis=1)


def y_step(planes, table_y):
    high, low = split(planes)
    products = dot(table_y, jnp.concatenate([high, low], axis=0))
    half = products.shape[0] // 2
    sums = products[:half] + products[half:]
    count = planes.shape[1] // NZ
    return jnp.concatenate(
        [
            jnp.concatenate(
                [sums[HI * k : HI * (k + 1), NZ * n : NZ * (n + 1)] for n in range(count)], axis=0
            )
            for k in range(2 * LO)
        ],
        axis=1,
    )


def y_step_back(rows, table_y):
    count = rows.shape[0] // HI
    stacked = jnp.concatenate(
        [
            jnp.concatenate(
                [rows[HI * n : HI * (n + 1), NZ * k : NZ * (k + 1)] for n in range(count)], axis=1
            )
            for k in range(2 * LO)
        ],
        axis=0,
    )
    return dot(table_y, rows3(stacked))


def put_modes(out_ref, products, channels, cells):
    for c in range(channels):
        rows = products[c * cells * HI : (c + 1) * cells * HI]
        for part in range(2):
            piece = rows[:, part * LANES : (part + 1) * LANES].reshape(cells, HI, LANES)
            out_ref[:, c, part * cells : (part + 1) * cells, :] = jnp.swapaxes(piece, 0, 1)


def take_modes(modes_ref, channels, cells):
    pieces = []
    for c in range(channels):
        parts = [
            jnp.swapaxes(modes_ref[:, c, part * cells : (part + 1) * cells, :], 0, 1).reshape(
                cells * HI, LANES
            )
            for part in range(2)
        ]
        pieces.append(jnp.concatenate(parts, axis=1))
    return jnp.concatenate(pieces, axis=0)


def channel_rows(c, cells):
    return pl.ds(pl.multiple_of(c * cells * HI, cells * HI), cells * HI)


def forward_kernel(channels, cells, field_ref, ty_ref, tz_ref, out_ref, left_ref):
    def body(c, carry):
        planes = jnp.concatenate([field_ref[0, c, x] for x in range(cells)], axis=1)
        left_ref[channel_rows(c, cells), :] = lanes3(y_step(planes, ty_ref[...]))
        return carry

    lax.fori_loop(0, channels, body, 0, unroll=2)
    put_modes(out_ref, dot(left_ref[...], tz_ref[...]), channels, cells)


def gelu_slope(x):
    return 0.5 * (1.0 + lax.erf(x * math.sqrt(0.5))) + x * (
        jnp.exp(-0.5 * x * x) * (1.0 / math.sqrt(2.0 * math.pi))
    )


def middle_kernel(
    channels, cells, modes_ref, point_ref, up_ref, tzi_ref, tyi_ref, ty_ref, tz_ref,
    grad_ref, out_ref, line_ref, left_ref,
):
    line_ref[...] = dot(lanes3(take_modes(modes_ref, channels, cells)), tzi_ref[...])

    def body(c, carry):
        rows = channel_rows(c, cells)
        spectral = y_step_back(line_ref[rows, :], tyi_ref[...])
        grads = []
        for x in range(cells):
            slope = gelu_slope(spectral[:, NZ * x : NZ * (x + 1)] + point_ref[0, c, x])
            grads.append(up_ref[0, c, x].astype(F32) * slope)
            grad_ref[0, c, x] = grads[x]
        left_ref[rows, :] = lanes3(y_step(jnp.concatenate(grads, axis=1), ty_ref[...]))
        return carry

    lax.fori_loop(0, channels, body, 0)
    put_modes(out_ref, dot(left_ref[...], tz_ref[...]), channels, cells)


def final_kernel(channels, cells, modes_ref, point_ref, tzi_ref, tyi_ref, out_ref, line_ref):
    line_ref[...] = dot(lanes3(take_modes(modes_ref, channels, cells)), tzi_ref[...])

    def body(c, carry):
        spectral = y_step_back(line_ref[channel_rows(c, cells), :], tyi_ref[...])
        for x in range(cells):
            out_ref[0, c, x] = spectral[:, NZ * x : NZ * (x + 1)] + point_ref[0, c, x]
        return carry

    lax.fori_loop(0, channels, body, 0, unroll=2)


def point_kernel(rows, field_ref, map_ref, bias_ref, *refs):
    out_ref = refs[-1]
    maps = map_ref[...]
    bias = bias_ref[...]
    channels = field_ref.shape[1]
    for r in range(0, rows, 16):
        pair = jnp.concatenate(
            [
                field_ref[0, :, 0, r : r + 8, :].reshape(channels * 8, NZ),
                field_ref[0, :, 0, r + 8 : r + 16, :].reshape(channels * 8, NZ),
            ],
            axis=1,
        )
        result = dot(maps, rows3(pair))
        out_ref[0, :, 0, r : r + 8, :] = (result[:, :NZ] + bias).reshape(channels, 8, NZ)
        out_ref[0, :, 0, r + 8 : r + 16, :] = (result[:, NZ:] + bias).reshape(channels, 8, NZ)


def whole(array):
    return pl.BlockSpec(array.shape, lambda *i: (0,) * array.ndim)


class Order:
    def __init__(self):
        self.token = None

    def call(self, kernel, operands, *, grid, in_specs, out_specs, out_shape, name, scratch=(), aliases=None, deps=()):
        many = isinstance(out_shape, (list, tuple))
        shapes = list(out_shape) if many else [out_shape]
        specs = list(out_specs) if many else [out_specs]
        count, outs = len(operands), len(shapes)
        first = self.token is None
        extra = ([] if first else [self.token]) + list(deps)
        anywhere = pl.BlockSpec(memory_space=pl.ANY)

        def body(*refs):
            given = count + len(extra)
            kernel(*refs[:count], *refs[given : given + outs], *refs[given + outs + 1 :])

        results = pl.pallas_call(
            body,
            grid=grid,
            in_specs=list(in_specs) + [anywhere] * len(extra),
            out_specs=specs + [anywhere],
            out_shape=shapes + [jax.ShapeDtypeStruct((8, 128), F32)],
            scratch_shapes=list(scratch),
            input_output_aliases=aliases or {},
            compiler_params=pltpu.CompilerParams(
                dimension_semantics=("arbitrary",) * len(grid), vmem_limit_bytes=VMEM_BYTES
            ),
            name=name,
        )(*operands, *extra)
        self.token = results[-1]
        return results[:-1] if many else results[0]


def forward_planes(order, fields, q, ty, tz):
    cells = fields.shape[2]
    per_chunk = fields.shape[1] // CHUNKS
    step = min(4, per_chunk)
    return order.call(
        partial(forward_kernel, step, cells),
        [fields, ty, tz],
        grid=(per_chunk // step,),
        in_specs=[
            pl.BlockSpec((1, step, cells, NY, NZ), lambda i: (0, q * (per_chunk // step) + i, 0, 0, 0)),
            whole(ty),
            whole(tz),
        ],
        out_specs=pl.BlockSpec((HI, step, 2 * cells, LANES), lambda i: (0, i, 0, 0)),
        out_shape=jax.ShapeDtypeStruct((HI, per_chunk, 2 * cells, LANES), F32),
        scratch=[pltpu.VMEM((step * cells * HI, 3 * 2 * LO * NZ), BF16)],
        name="planes_to_modes",
    )


def middle_planes(order, modes, point, upstream, q, tzi, tyi, ty, tz):
    cells = point.shape[2]
    per_chunk = point.shape[1] // CHUNKS
    step = min(4, per_chunk)
    modes_spec = pl.BlockSpec((HI, step, 2 * cells, LANES), lambda i: (0, i, 0, 0))
    cells_spec = pl.BlockSpec(
        (1, step, cells, NY, NZ), lambda i: (0, q * (per_chunk // step) + i, 0, 0, 0)
    )
    return order.call(
        partial(middle_kernel, step, cells),
        [modes, point, upstream, tzi, tyi, ty, tz],
        grid=(per_chunk // step,),
        in_specs=[modes_spec, cells_spec, cells_spec, whole(tzi), whole(tyi), whole(ty), whole(tz)],
        out_specs=[cells_spec, modes_spec],
        out_shape=[
            jax.ShapeDtypeStruct(point.shape, F32),
            jax.ShapeDtypeStruct((HI, per_chunk, 2 * cells, LANES), F32),
        ],
        scratch=[
            pltpu.VMEM((step * cells * HI, 2 * LO * NZ), F32),
            pltpu.VMEM((step * cells * HI, 3 * 2 * LO * NZ), BF16),
        ],
        aliases={1: 0},
        name="modes_to_gradient_to_modes",
    )


def final_planes(order, modes, point, q, tzi, tyi):
    cells = point.shape[2]
    per_chunk = point.shape[1] // CHUNKS
    step = min(4, per_chunk)
    cells_spec = pl.BlockSpec(
        (1, step, cells, NY, NZ), lambda i: (0, q * (per_chunk // step) + i, 0, 0, 0)
    )
    return order.call(
        partial(final_kernel, step, cells),
        [modes, point, tzi, tyi],
        grid=(per_chunk // step,),
        in_specs=[
            pl.BlockSpec((HI, step, 2 * cells, LANES), lambda i: (0, i, 0, 0)),
            cells_spec,
            whole(tzi),
            whole(tyi),
        ],
        out_specs=cells_spec,
        out_shape=jax.ShapeDtypeStruct(point.shape, F32),
        scratch=[pltpu.VMEM((step * cells * HI, 2 * LO * NZ), F32)],
        aliases={1: 0},
        name="modes_to_planes",
    )


def point_table_kernel(weight_ref, spread_ref, out_ref):
    spread = spread_ref[...]
    size = spread.shape[0]
    row = lax.broadcasted_iota(jnp.int32, (size, size), 0)
    column = lax.broadcasted_iota(jnp.int32, (size, size), 1)
    same = jnp.bitwise_and(row, 7) == jnp.bitwise_and(column, 7)
    parts = []
    for part in split(weight_ref[...]):
        left = dot(spread, part).astype(BF16)
        full = lax.dot_general(left, spread, (((1,), (1,)), ((), ())), preferred_element_type=F32)
        parts.append(jnp.where(same, full, 0.0).astype(BF16))
    out_ref[...] = jnp.concatenate([parts[0], parts[0], parts[1]], axis=1)


def point_tables(weight, bias):
    channels = bias.shape[0]
    spread = np.repeat(np.eye(channels), 8, axis=0).astype(ml_dtypes.bfloat16)
    mapping = pl.pallas_call(
        point_table_kernel,
        out_shape=jax.ShapeDtypeStruct((channels * 8, channels * 8 * 3), BF16),
        name="channel_table",
    )(weight.T, jnp.asarray(spread))
    return mapping, jnp.broadcast_to(jnp.repeat(bias, 8)[:, None], (channels * 8, NZ))


def point_map(order, fields, tables, q, buffer, deps=()):
    channels, cells = fields.shape[1], fields.shape[2]
    rows = NY
    part = cells // PARTS
    mapping, shift = tables
    spec = pl.BlockSpec((1, channels, 1, rows, NZ), lambda i, j: (0, 0, q * part + i, j, 0))
    operands = [fields, mapping, shift]
    specs = [spec, whole(mapping), whole(shift)]
    aliases = {}
    if buffer is not None:
        operands.append(buffer)
        specs.append(pl.BlockSpec(memory_space=pl.ANY))
        aliases = {3: 0}
    return order.call(
        partial(point_kernel, rows),
        [*operands],
        grid=(part, NY // rows),
        in_specs=specs,
        out_specs=spec,
        out_shape=jax.ShapeDtypeStruct(fields.shape, F32),
        aliases=aliases,
        deps=deps,
        name="channel_map",
    )


def channel_pairs(refs, channels):
    for c in range(0, channels, 2):
        yield c, jnp.concatenate(
            [
                jnp.concatenate([ref[:, c + k].reshape(-1, ref.shape[-1]) for ref in refs], axis=0)
                for k in range(2)
            ],
            axis=1,
        )


def line_send_kernel(data_ref, table_ref, out_ref):
    lanes = data_ref.shape[-1]
    for c, pair in channel_pairs([data_ref.at[:, 0]], data_ref.shape[2]):
        result = dot(table_ref[...], rows3(pair))
        for k in range(2):
            out_ref[c + k] = result[:, k * lanes : (k + 1) * lanes]


def line_keep_kernel(data_ref, other_ref, table_ref, *out_refs):
    lanes = data_ref.shape[-1]
    rows = out_refs[0].shape[1]
    for c, pair in channel_pairs([data_ref.at[:, 0]], data_ref.shape[2]):
        result = dot(table_ref[...], rows3(pair))
        for k in range(2):
            total = result[:, k * lanes : (k + 1) * lanes] + other_ref[c + k]
            for g, out_ref in enumerate(out_refs):
                out_ref[c + k] = total[g * rows : (g + 1) * rows]


def line_send(order, data, table):
    near, _, channels, rows, lanes = data.shape
    modes = table.shape[0]
    step = min(8, channels)
    return order.call(
        line_send_kernel,
        [data, table],
        grid=(channels // step,),
        in_specs=[
            pl.BlockSpec((near, 1, step, rows, lanes), lambda i: (0, 1, i, 0, 0)),
            whole(table),
        ],
        out_specs=pl.BlockSpec((step, modes, lanes), lambda i: (i, 0, 0)),
        out_shape=jax.ShapeDtypeStruct((channels, modes, lanes), F32),
        name="partner_modes",
    )


def line_keep(order, data, other, table, groups):
    near, _, channels, rows, lanes = data.shape
    modes = table.shape[0]
    step = min(8, channels)
    return order.call(
        line_keep_kernel,
        [data, other, table],
        grid=(channels // step,),
        in_specs=[
            pl.BlockSpec((near, 1, step, rows, lanes), lambda i: (0, 0, i, 0, 0)),
            pl.BlockSpec((step, modes, lanes), lambda i: (i, 0, 0)),
            whole(table),
        ],
        out_specs=[pl.BlockSpec((step, modes // groups, lanes), lambda i: (i, 0, 0))] * groups,
        out_shape=[jax.ShapeDtypeStruct((channels, modes // groups, lanes), F32)] * groups,
        name="own_modes",
    )


def line_back_kernel(own_ref, other_ref, table_ref, out_ref):
    lanes = own_ref.shape[-1]
    near, _, channels, rows, _ = out_ref.shape
    for part, ref in enumerate((own_ref, other_ref)):
        for c, pair in channel_pairs([ref], channels):
            result = dot(table_ref[...], rows3(pair))
            for k in range(2):
                out_ref[:, part, c + k] = result[:, k * lanes : (k + 1) * lanes].reshape(
                    near, rows, lanes
                )


def line_back(order, own, other, table, near, deps=()):
    groups, channels, rows, lanes = own.shape
    step = min(8, channels)
    rows_out = table.shape[0] // near
    return order.call(
        line_back_kernel,
        [own, other, table],
        grid=(channels // step,),
        in_specs=[pl.BlockSpec((groups, step, rows, lanes), lambda i: (0, i, 0, 0))] * 2
        + [whole(table)],
        out_specs=pl.BlockSpec((near, 2, step, rows_out, lanes), lambda i: (0, 0, i, 0, 0)),
        out_shape=jax.ShapeDtypeStruct((near, 2, channels, rows_out, lanes), F32),
        deps=deps,
        name="modes_to_cells",
    )


def mix_kernel(adjoint, groups, *refs):
    spec_refs, weight_ref, out_refs = refs[: CHUNKS * groups], refs[CHUNKS * groups], refs[-groups:]
    per_chunk = spec_refs[0].shape[0]
    rows = out_refs[0].shape[1] // 2
    for o in range(out_refs[0].shape[0]):
        real = [None] * groups
        imag = [None] * groups
        for i in range(CHUNKS * per_chunk):
            at = (o, i) if adjoint else (i, o)
            wr, wi = weight_ref[0, at[0], at[1]], weight_ref[1, at[0], at[1]]
            for s in range(groups):
                spec_ref = spec_refs[(i // per_chunk) * groups + s]
                sr = spec_ref[i % per_chunk, :rows]
                si = spec_ref[i % per_chunk, rows:]
                if adjoint:
                    re, im = wr * sr + wi * si, wr * si - wi * sr
                else:
                    re, im = wr * sr - wi * si, wr * si + wi * sr
                real[s] = re if i == 0 else real[s] + re
                imag[s] = im if i == 0 else imag[s] + im
        for s in range(groups):
            out_refs[s][o, :rows] = real[s]
            out_refs[s][o, rows:] = imag[s]


def mix(order, spectra, weight, q, adjoint):
    groups = len(spectra[0])
    per_chunk, rows, lanes = spectra[0][0].shape
    channels = weight.shape[1]
    step = 4
    if adjoint:
        block = (2, step, channels, rows // 2, lanes)
        place = lambda i: (0, q * (per_chunk // step) + i, 0, 0, 0)
    else:
        block = (2, channels, step, rows // 2, lanes)
        place = lambda i: (0, 0, q * (per_chunk // step) + i, 0, 0)
    flat = [piece for chunk in spectra for piece in chunk]
    return order.call(
        partial(mix_kernel, adjoint, groups),
        [*flat, weight],
        grid=(per_chunk // step,),
        in_specs=[whole(s) for s in flat] + [pl.BlockSpec(block, place)],
        out_specs=[pl.BlockSpec((step, rows, lanes), lambda i: (i, 0, 0))] * groups,
        out_shape=[jax.ShapeDtypeStruct((per_chunk, rows, lanes), F32)] * groups,
        name="mix_back" if adjoint else "mix",
    )


def weight_kernel(groups, *refs):
    grad_refs, spec_refs, out_ref = refs[: CHUNKS * groups], refs[CHUNKS * groups : -1], refs[-1]
    per_chunk = grad_refs[0].shape[0]
    rows = grad_refs[0].shape[1] // 2
    for i in range(out_ref.shape[1]):
        sr = [spec_refs[s][i, :rows] for s in range(groups)]
        si = [spec_refs[s][i, rows:] for s in range(groups)]
        for o in range(out_ref.shape[2]):
            real = imag = None
            for s in range(groups):
                grad_ref = grad_refs[(o // per_chunk) * groups + s]
                gr = grad_ref[o % per_chunk, :rows]
                gi = grad_ref[o % per_chunk, rows:]
                re, im = gr * sr[s] + gi * si[s], gi * sr[s] - gr * si[s]
                real = re if s == 0 else real + re
                imag = im if s == 0 else imag + im
            out_ref[0, i, o] = real
            out_ref[1, i, o] = imag


def weight_gradient(order, gradients, spectra, q, buffer, deps=()):
    groups = len(spectra)
    per_chunk, rows, lanes = spectra[0].shape
    channels = per_chunk * CHUNKS
    step = 2
    flat = [piece for chunk in gradients for piece in chunk]
    operands = flat + list(spectra)
    specs = [whole(g) for g in flat] + [
        pl.BlockSpec((step, rows, lanes), lambda i: (i, 0, 0)) for _ in spectra
    ]
    aliases = {}
    kernel = partial(weight_kernel, groups)
    if buffer is not None:
        aliases = {len(operands): 0}
        operands = operands + [buffer]
        specs = specs + [pl.BlockSpec(memory_space=pl.ANY)]
        kernel = lambda *refs: weight_kernel(groups, *refs[:-2], refs[-1])
    return order.call(
        kernel,
        [*operands],
        grid=(per_chunk // step,),
        in_specs=specs,
        out_specs=pl.BlockSpec(
            (2, step, channels, rows // 2, lanes),
            lambda i: (0, q * (per_chunk // step) + i, 0, 0, 0),
        ),
        out_shape=jax.ShapeDtypeStruct((2, channels, channels, rows // 2, lanes), F32),
        aliases=aliases,
        deps=deps,
        name="weight_gradient",
    )


def cut_lanes(modes, slabs):
    parts = slabs // HI
    if parts == 1:
        return modes
    _, channels, rows, lanes = modes.shape
    cut = modes.reshape(HI, channels, rows, parts, lanes // parts)
    return cut.transpose(0, 3, 1, 2, 4).reshape(slabs, channels, rows, lanes // parts)


def join_lanes(modes, slabs):
    parts = slabs // HI
    if parts == 1:
        return modes
    _, channels, rows, lanes = modes.shape
    cut = modes.reshape(HI, parts, channels, rows, lanes)
    return cut.transpose(0, 2, 3, 1, 4).reshape(HI, channels, rows, lanes * parts)


def shards(groups, slabs, fields, upstream, spectral_weight, point_weight, point_bias):
    near = slabs // 2
    half = lax.axis_index("mp") // near
    group = lax.axis_index("dp")

    def pick(tables, index):
        return lax.dynamic_index_in_dim(jnp.asarray(np.stack(tables)), index, 0, False)

    both = [(h, g) for h in range(2) for g in range(groups)]
    tx = pick([x_forward(groups, slabs, h, g) for h, g in both], half * groups + group)
    txi = pick([x_inverse(groups, slabs, h, g) for h, g in both], half * groups + group)
    ty = pick([y_forward(slabs, h) for h in range(2)], half)
    tyi = pick([y_inverse(slabs, h) for h in range(2)], half)
    tz, tz_scaled = jnp.asarray(z_forward(False)), jnp.asarray(z_forward(True))
    tzi, tzi_scaled = jnp.asarray(z_inverse(False)), jnp.asarray(z_inverse(True))
    halves = [[h * near + d for d in range(near)] for h in range(2)]
    across = [(j, j ^ near) for j in range(slabs)]

    def swap_near(data):
        return lax.all_to_all(
            data, "mp", split_axis=0, concat_axis=0, axis_index_groups=halves, tiled=True
        )

    def swap_groups(pieces):
        return [pieces[0]] + [
            lax.ppermute(pieces[k], "dp", [(j, j ^ k) for j in range(groups)])
            for k in range(1, groups)
        ]

    def near_blocks(planes):
        cut = cut_lanes(planes, slabs)
        return swap_near(cut.reshape((near, 2) + cut.shape[1:]))

    point = point_tables(point_weight, point_bias)
    point_back = point_tables(point_weight.T, jnp.zeros_like(point_bias))
    order = Order()
    state = {}

    def forward(q):
        planes = forward_planes(order, fields, q, ty, tz)
        state["near", q] = near_blocks(planes)

    def send(q):
        state["other", q] = lax.ppermute(line_send(order, state["near", q], tx), "mp", across)

    def keep(q):
        pieces = line_keep(order, state["near", q], state["other", q], tx, groups)
        state["spectrum", q] = swap_groups(pieces)

    def mixed(q, spectra, adjoint):
        own = jnp.stack(swap_groups(mix(order, spectra, spectral_weight, q, adjoint)))
        state["own", q] = own, lax.ppermute(own, "mp", across)

    def back(q, *deps):
        cells = swap_near(line_back(order, *state["own", q], txi, near, deps))
        state["planes", q] = join_lanes(cells.reshape((slabs,) + cells.shape[2:]), slabs)

    def channels(source, tables, key, q, *deps):
        state[key] = point_map(order, source, tables, q, state.get(key), deps)

    def middle(q):
        state["point"], planes = middle_planes(
            order, state["planes", q], state["point"], upstream, q, tzi_scaled, tyi, ty, tz_scaled
        )
        state["near", q] = near_blocks(planes)

    def weights(q, *deps):
        state["weights"] = weight_gradient(
            order, gradients, spectra[q], q, state.get("weights"), deps
        )

    def final(q):
        state["result"] = final_planes(order, state["planes", q], state["result"], q, tzi, tyi)

    map_fields = partial(channels, fields, point, "point")
    forward(0)
    forward(1)
    map_fields(0)
    map_fields(1)
    send(0)
    map_fields(2)
    send(1)
    keep(0)
    map_fields(3)
    keep(1)
    spectra = [state["spectrum", q] for q in range(CHUNKS)]
    mixed(0, spectra, False)
    mixed(1, spectra, False)
    back(0, state["own", 1][0])
    back(1)
    middle(0)
    middle(1)
    map_back = partial(channels, state["point"], point_back, "result")
    send(0)
    map_back(0)
    map_back(1)
    send(1)
    keep(0)
    map_back(2)
    map_back(3)
    keep(1)
    gradients = [state["spectrum", q] for q in range(CHUNKS)]
    mixed(0, gradients, True)
    mixed(1, gradients, True)
    weights(0, state["own", 0][0], state["own", 1][0])
    back(0)
    weights(1)
    back(1)
    final(0)
    final(1)
    return state["result"], state["weights"]


def solution(mesh):
    placed = (
        P("dp", None, "mp", None, None),
        P("dp", None, "mp", None, None),
        P(None, None, None, "dp", "mp"),
        P(),
        P(),
    )
    return jax.shard_map(
        partial(shards, mesh.shape["dp"], mesh.shape["mp"]),
        mesh=mesh,
        in_specs=placed,
        out_specs=(P("dp", None, "mp", None, None), P(None, None, None, "dp", "mp")),
        check_vma=False,
    )
```

```python
from functools import partial
import math

import jax
import jax.numpy as jnp
import ml_dtypes
import numpy as np
from jax import lax
from jax.experimental import pallas as pl
from jax.experimental.pallas import tpu as pltpu
from jax.sharding import PartitionSpec as P

NX = 128
NY = 128
NZ = 128
MX = 32
MY = 32
MZ = 32
CELLS = NX * NY * NZ
HI = 8
LO = MY // HI
LANES = LO * MZ
CHUNKS = 2
PARTS = 4
F32 = jnp.float32
BF16 = jnp.bfloat16
VMEM_BYTES = 56 * 1024 * 1024


def signed(j, kept):
    return np.where(j < kept // 2, j, j - kept)


def second_order(slabs, half):
    parts = slabs // HI
    each = LO // parts
    at = np.arange(MY).reshape(HI, LO)
    place = (at // LO) * parts + (at % LO) // each
    slab = ((place % 2) ^ half) * (slabs // 2) + place // 2
    return slab * each + at % each


def waves(number, frequencies):
    phases = np.mod(np.arange(number)[:, None] * frequencies[None, :], number) * (2.0 * np.pi / number)
    return np.cos(phases), np.sin(phases)


def two_parts(table):
    high = table.astype(ml_dtypes.bfloat16)
    low = (table - high.astype(np.float64)).astype(ml_dtypes.bfloat16)
    return high, low


def stack_left(table):
    high, low = two_parts(table)
    return np.concatenate([high, high, low], axis=1)


def stack_right(table):
    high, low = two_parts(table)
    return np.concatenate([high, high, low], axis=0)


def y_forward(slabs, half):
    cos, sin = waves(NY, signed(np.arange(MY), MY))
    order = second_order(slabs, half)
    rows = np.stack([cos[:, order], sin[:, order]], axis=0)
    table = rows.transpose(3, 0, 2, 1).reshape(LO * 2 * HI, NY)
    high, low = two_parts(table)
    top = np.concatenate([high, high], axis=1)
    bottom = np.concatenate([low, np.zeros_like(low)], axis=1)
    return np.concatenate([top, bottom], axis=0)


def y_inverse(slabs, half):
    cos, sin = waves(NY, signed(np.arange(MY), MY))
    order = second_order(slabs, half)
    rows = np.stack([cos[:, order], -sin[:, order]], axis=0)
    return stack_left(rows.transpose(1, 3, 0, 2).reshape(NY, LO * 2 * HI))


def mode_factor():
    return np.where(np.arange(MZ) == 0, 1.0, 2.0) / CELLS


def z_forward(scaled):
    cos, sin = waves(NZ, np.arange(MZ))
    scale = mode_factor() if scaled else np.ones(MZ)
    small = np.zeros((2, NZ, 2, MZ))
    small[0, :, 0] = cos * scale
    small[1, :, 0] = -sin * scale
    small[0, :, 1] = -sin * scale
    small[1, :, 1] = -cos * scale
    table = np.zeros((LO, 2, NZ, 2, LO, MZ))
    for a in range(LO):
        table[a, :, :, :, a, :] = small
    return stack_right(table.reshape(LO * 2 * NZ, 2 * LANES))


def z_inverse(scaled):
    cos, sin = waves(NZ, np.arange(MZ))
    scale = mode_factor() if scaled else np.ones(MZ)
    small = np.zeros((2, MZ, 2, NZ))
    small[0, :, 0] = (cos * scale).T
    small[1, :, 0] = (-sin * scale).T
    small[0, :, 1] = (sin * scale).T
    small[1, :, 1] = (cos * scale).T
    table = np.zeros((2, LO, MZ, LO, 2, NZ))
    for a in range(LO):
        table[:, a, :, a, :, :] = small
    return stack_right(table.reshape(2 * LANES, LO * 2 * NZ))


def x_table(groups, slabs, half, group):
    cos, sin = waves(NX, signed(np.arange(MX), MX))
    near = slabs // 2
    cells = NX // slabs
    order = np.arange(MX).reshape(groups, MX // groups)[np.arange(groups) ^ group]
    rows = slice(half * (NX // 2), (half + 1) * (NX // 2))
    return [t[rows][:, order].reshape(near, cells, groups, MX // groups) for t in (cos, sin)]


def x_forward(groups, slabs, half, group):
    cos, sin = [t.transpose(2, 3, 0, 1) for t in x_table(groups, slabs, half, group)]
    table = np.zeros((groups, 2, MX // groups, slabs // 2, 2, NX // slabs))
    table[:, 0, :, :, 0] = cos
    table[:, 0, :, :, 1] = sin
    table[:, 1, :, :, 0] = -sin
    table[:, 1, :, :, 1] = cos
    return stack_left(table.reshape(2 * MX, NX))


def x_inverse(groups, slabs, half, group):
    cos, sin = [t.transpose(0, 1, 2, 3) for t in x_table(groups, slabs, half, group)]
    table = np.zeros((slabs // 2, 2, NX // slabs, groups, 2, MX // groups))
    table[:, 0, :, :, 0] = cos
    table[:, 0, :, :, 1] = -sin
    table[:, 1, :, :, 0] = sin
    table[:, 1, :, :, 1] = cos
    return stack_left(table.reshape(NX, 2 * MX))


def split(values):
    high = values.astype(BF16)
    return high, (values - high.astype(F32)).astype(BF16)


def dot(left, right):
    return jnp.dot(left, right, preferred_element_type=F32)


def rows3(values):
    high, low = split(values)
    return jnp.concatenate([high, low, high], axis=0)


def lanes3(values):
    high, low = split(values)
    return jnp.concatenate([high, low, high], axis=1)


def y_step(planes, table_y):
    high, low = split(planes)
    products = dot(table_y, jnp.concatenate([high, low], axis=0))
    half = products.shape[0] // 2
    sums = products[:half] + products[half:]
    count = planes.shape[1] // NZ
    return jnp.concatenate(
        [
            jnp.concatenate(
                [sums[HI * k : HI * (k + 1), NZ * n : NZ * (n + 1)] for n in range(count)], axis=0
            )
            for k in range(2 * LO)
        ],
        axis=1,
    )


def y_step_back(rows, table_y):
    count = rows.shape[0] // HI
    stacked = jnp.concatenate(
        [
            jnp.concatenate(
                [rows[HI * n : HI * (n + 1), NZ * k : NZ * (k + 1)] for n in range(count)], axis=1
            )
            for k in range(2 * LO)
        ],
        axis=0,
    )
    return dot(table_y, rows3(stacked))


def put_modes(out_ref, products, channels, cells):
    for c in range(channels):
        rows = products[c * cells * HI : (c + 1) * cells * HI]
        for part in range(2):
            piece = rows[:, part * LANES : (part + 1) * LANES].reshape(cells, HI, LANES)
            out_ref[:, c, part * cells : (part + 1) * cells, :] = jnp.swapaxes(piece, 0, 1)


def take_modes(modes_ref, channels, cells):
    pieces = []
    for c in range(channels):
        parts = [
            jnp.swapaxes(modes_ref[:, c, part * cells : (part + 1) * cells, :], 0, 1).reshape(
                cells * HI, LANES
            )
            for part in range(2)
        ]
        pieces.append(jnp.concatenate(parts, axis=1))
    return jnp.concatenate(pieces, axis=0)


def channel_rows(c, cells):
    return pl.ds(pl.multiple_of(c * cells * HI, cells * HI), cells * HI)


def forward_kernel(channels, cells, field_ref, ty_ref, tz_ref, out_ref, left_ref):
    def body(c, carry):
        planes = jnp.concatenate([field_ref[0, c, x] for x in range(cells)], axis=1)
        left_ref[channel_rows(c, cells), :] = lanes3(y_step(planes, ty_ref[...]))
        return carry

    lax.fori_loop(0, channels, body, 0, unroll=2)
    put_modes(out_ref, dot(left_ref[...], tz_ref[...]), channels, cells)


def gelu_slope(x):
    return 0.5 * (1.0 + lax.erf(x * math.sqrt(0.5))) + x * (
        jnp.exp(-0.5 * x * x) * (1.0 / math.sqrt(2.0 * math.pi))
    )


def middle_kernel(
    channels, cells, modes_ref, point_ref, up_ref, tzi_ref, tyi_ref, ty_ref, tz_ref,
    grad_ref, out_ref, line_ref, left_ref,
):
    line_ref[...] = dot(lanes3(take_modes(modes_ref, channels, cells)), tzi_ref[...])

    def body(c, carry):
        rows = channel_rows(c, cells)
        spectral = y_step_back(line_ref[rows, :], tyi_ref[...])
        grads = []
        for x in range(cells):
            slope = gelu_slope(spectral[:, NZ * x : NZ * (x + 1)] + point_ref[0, c, x])
            grads.append(up_ref[0, c, x].astype(F32) * slope)
            grad_ref[0, c, x] = grads[x]
        left_ref[rows, :] = lanes3(y_step(jnp.concatenate(grads, axis=1), ty_ref[...]))
        return carry

    lax.fori_loop(0, channels, body, 0)
    put_modes(out_ref, dot(left_ref[...], tz_ref[...]), channels, cells)


def final_kernel(channels, cells, modes_ref, point_ref, tzi_ref, tyi_ref, out_ref, line_ref):
    line_ref[...] = dot(lanes3(take_modes(modes_ref, channels, cells)), tzi_ref[...])

    def body(c, carry):
        spectral = y_step_back(line_ref[channel_rows(c, cells), :], tyi_ref[...])
        for x in range(cells):
            out_ref[0, c, x] = spectral[:, NZ * x : NZ * (x + 1)] + point_ref[0, c, x]
        return carry

    lax.fori_loop(0, channels, body, 0, unroll=2)


def point_kernel(rows, field_ref, map_ref, bias_ref, *refs):
    out_ref = refs[-1]
    maps = map_ref[...]
    bias = bias_ref[...]
    channels = field_ref.shape[1]
    for r in range(0, rows, 16):
        pair = jnp.concatenate(
            [
                field_ref[0, :, 0, r : r + 8, :].reshape(channels * 8, NZ),
                field_ref[0, :, 0, r + 8 : r + 16, :].reshape(channels * 8, NZ),
            ],
            axis=1,
        )
        result = dot(maps, rows3(pair))
        out_ref[0, :, 0, r : r + 8, :] = (result[:, :NZ] + bias).reshape(channels, 8, NZ)
        out_ref[0, :, 0, r + 8 : r + 16, :] = (result[:, NZ:] + bias).reshape(channels, 8, NZ)


def whole(array):
    return pl.BlockSpec(array.shape, lambda *i: (0,) * array.ndim)


class Order:
    def __init__(self):
        self.token = None

    def call(self, kernel, operands, *, grid, in_specs, out_specs, out_shape, name, scratch=(), aliases=None, deps=()):
        many = isinstance(out_shape, (list, tuple))
        shapes = list(out_shape) if many else [out_shape]
        specs = list(out_specs) if many else [out_specs]
        count, outs = len(operands), len(shapes)
        first = self.token is None
        extra = ([] if first else [self.token]) + list(deps)
        anywhere = pl.BlockSpec(memory_space=pl.ANY)

        def body(*refs):
            given = count + len(extra)
            kernel(*refs[:count], *refs[given : given + outs], *refs[given + outs + 1 :])

        results = pl.pallas_call(
            body,
            grid=grid,
            in_specs=list(in_specs) + [anywhere] * len(extra),
            out_specs=specs + [anywhere],
            out_shape=shapes + [jax.ShapeDtypeStruct((8, 128), F32)],
            scratch_shapes=list(scratch),
            input_output_aliases=aliases or {},
            compiler_params=pltpu.CompilerParams(
                dimension_semantics=("arbitrary",) * len(grid), vmem_limit_bytes=VMEM_BYTES
            ),
            name=name,
        )(*operands, *extra)
        self.token = results[-1]
        return results[:-1] if many else results[0]


def forward_planes(order, fields, q, ty, tz):
    cells = fields.shape[2]
    per_chunk = fields.shape[1] // CHUNKS
    step = min(4, per_chunk)
    return order.call(
        partial(forward_kernel, step, cells),
        [fields, ty, tz],
        grid=(per_chunk // step,),
        in_specs=[
            pl.BlockSpec((1, step, cells, NY, NZ), lambda i: (0, q * (per_chunk // step) + i, 0, 0, 0)),
            whole(ty),
            whole(tz),
        ],
        out_specs=pl.BlockSpec((HI, step, 2 * cells, LANES), lambda i: (0, i, 0, 0)),
        out_shape=jax.ShapeDtypeStruct((HI, per_chunk, 2 * cells, LANES), F32),
        scratch=[pltpu.VMEM((step * cells * HI, 3 * 2 * LO * NZ), BF16)],
        name="planes_to_modes",
    )


def middle_planes(order, modes, point, upstream, q, tzi, tyi, ty, tz):
    cells = point.shape[2]
    per_chunk = point.shape[1] // CHUNKS
    step = min(4, per_chunk)
    modes_spec = pl.BlockSpec((HI, step, 2 * cells, LANES), lambda i: (0, i, 0, 0))
    cells_spec = pl.BlockSpec(
        (1, step, cells, NY, NZ), lambda i: (0, q * (per_chunk // step) + i, 0, 0, 0)
    )
    return order.call(
        partial(middle_kernel, step, cells),
        [modes, point, upstream, tzi, tyi, ty, tz],
        grid=(per_chunk // step,),
        in_specs=[modes_spec, cells_spec, cells_spec, whole(tzi), whole(tyi), whole(ty), whole(tz)],
        out_specs=[cells_spec, modes_spec],
        out_shape=[
            jax.ShapeDtypeStruct(point.shape, F32),
            jax.ShapeDtypeStruct((HI, per_chunk, 2 * cells, LANES), F32),
        ],
        scratch=[
            pltpu.VMEM((step * cells * HI, 2 * LO * NZ), F32),
            pltpu.VMEM((step * cells * HI, 3 * 2 * LO * NZ), BF16),
        ],
        aliases={1: 0},
        name="modes_to_gradient_to_modes",
    )


def final_planes(order, modes, point, q, tzi, tyi):
    cells = point.shape[2]
    per_chunk = point.shape[1] // CHUNKS
    step = min(4, per_chunk)
    cells_spec = pl.BlockSpec(
        (1, step, cells, NY, NZ), lambda i: (0, q * (per_chunk // step) + i, 0, 0, 0)
    )
    return order.call(
        partial(final_kernel, step, cells),
        [modes, point, tzi, tyi],
        grid=(per_chunk // step,),
        in_specs=[
            pl.BlockSpec((HI, step, 2 * cells, LANES), lambda i: (0, i, 0, 0)),
            cells_spec,
            whole(tzi),
            whole(tyi),
        ],
        out_specs=cells_spec,
        out_shape=jax.ShapeDtypeStruct(point.shape, F32),
        scratch=[pltpu.VMEM((step * cells * HI, 2 * LO * NZ), F32)],
        aliases={1: 0},
        name="modes_to_planes",
    )


def point_table_kernel(weight_ref, spread_ref, out_ref):
    spread = spread_ref[...]
    size = spread.shape[0]
    row = lax.broadcasted_iota(jnp.int32, (size, size), 0)
    column = lax.broadcasted_iota(jnp.int32, (size, size), 1)
    same = jnp.bitwise_and(row, 7) == jnp.bitwise_and(column, 7)
    parts = []
    for part in split(weight_ref[...]):
        left = dot(spread, part).astype(BF16)
        full = lax.dot_general(left, spread, (((1,), (1,)), ((), ())), preferred_element_type=F32)
        parts.append(jnp.where(same, full, 0.0).astype(BF16))
    out_ref[...] = jnp.concatenate([parts[0], parts[0], parts[1]], axis=1)


def point_tables(weight, bias):
    channels = bias.shape[0]
    spread = np.repeat(np.eye(channels), 8, axis=0).astype(ml_dtypes.bfloat16)
    mapping = pl.pallas_call(
        point_table_kernel,
        out_shape=jax.ShapeDtypeStruct((channels * 8, channels * 8 * 3), BF16),
        name="channel_table",
    )(weight.T, jnp.asarray(spread))
    return mapping, jnp.broadcast_to(jnp.repeat(bias, 8)[:, None], (channels * 8, NZ))


def point_map(order, fields, tables, q, buffer, deps=()):
    channels, cells = fields.shape[1], fields.shape[2]
    rows = NY
    part = cells // PARTS
    mapping, shift = tables
    spec = pl.BlockSpec((1, channels, 1, rows, NZ), lambda i, j: (0, 0, q * part + i, j, 0))
    operands = [fields, mapping, shift]
    specs = [spec, whole(mapping), whole(shift)]
    aliases = {}
    if buffer is not None:
        operands.append(buffer)
        specs.append(pl.BlockSpec(memory_space=pl.ANY))
        aliases = {3: 0}
    return order.call(
        partial(point_kernel, rows),
        [*operands],
        grid=(part, NY // rows),
        in_specs=specs,
        out_specs=spec,
        out_shape=jax.ShapeDtypeStruct(fields.shape, F32),
        aliases=aliases,
        deps=deps,
        name="channel_map",
    )


def channel_pairs(refs, channels):
    for c in range(0, channels, 2):
        yield c, jnp.concatenate(
            [
                jnp.concatenate([ref[:, c + k].reshape(-1, ref.shape[-1]) for ref in refs], axis=0)
                for k in range(2)
            ],
            axis=1,
        )


def line_send_kernel(data_ref, table_ref, out_ref):
    lanes = data_ref.shape[-1]
    for c, pair in channel_pairs([data_ref.at[:, 0]], data_ref.shape[2]):
        result = dot(table_ref[...], rows3(pair))
        for k in range(2):
            out_ref[c + k] = result[:, k * lanes : (k + 1) * lanes]


def line_keep_kernel(data_ref, other_ref, table_ref, *out_refs):
    lanes = data_ref.shape[-1]
    rows = out_refs[0].shape[1]
    for c, pair in channel_pairs([data_ref.at[:, 0]], data_ref.shape[2]):
        result = dot(table_ref[...], rows3(pair))
        for k in range(2):
            total = result[:, k * lanes : (k + 1) * lanes] + other_ref[c + k]
            for g, out_ref in enumerate(out_refs):
                out_ref[c + k] = total[g * rows : (g + 1) * rows]


def line_send(order, data, table):
    near, _, channels, rows, lanes = data.shape
    modes = table.shape[0]
    step = min(8, channels)
    return order.call(
        line_send_kernel,
        [data, table],
        grid=(channels // step,),
        in_specs=[
            pl.BlockSpec((near, 1, step, rows, lanes), lambda i: (0, 1, i, 0, 0)),
            whole(table),
        ],
        out_specs=pl.BlockSpec((step, modes, lanes), lambda i: (i, 0, 0)),
        out_shape=jax.ShapeDtypeStruct((channels, modes, lanes), F32),
        name="partner_modes",
    )


def line_keep(order, data, other, table, groups):
    near, _, channels, rows, lanes = data.shape
    modes = table.shape[0]
    step = min(8, channels)
    return order.call(
        line_keep_kernel,
        [data, other, table],
        grid=(channels // step,),
        in_specs=[
            pl.BlockSpec((near, 1, step, rows, lanes), lambda i: (0, 0, i, 0, 0)),
            pl.BlockSpec((step, modes, lanes), lambda i: (i, 0, 0)),
            whole(table),
        ],
        out_specs=[pl.BlockSpec((step, modes // groups, lanes), lambda i: (i, 0, 0))] * groups,
        out_shape=[jax.ShapeDtypeStruct((channels, modes // groups, lanes), F32)] * groups,
        name="own_modes",
    )


def line_back_kernel(own_ref, other_ref, table_ref, out_ref):
    lanes = own_ref.shape[-1]
    near, _, channels, rows, _ = out_ref.shape
    for part, ref in enumerate((own_ref, other_ref)):
        for c, pair in channel_pairs([ref], channels):
            result = dot(table_ref[...], rows3(pair))
            for k in range(2):
                out_ref[:, part, c + k] = result[:, k * lanes : (k + 1) * lanes].reshape(
                    near, rows, lanes
                )


def line_back(order, own, other, table, near, deps=()):
    groups, channels, rows, lanes = own.shape
    step = min(8, channels)
    rows_out = table.shape[0] // near
    return order.call(
        line_back_kernel,
        [own, other, table],
        grid=(channels // step,),
        in_specs=[pl.BlockSpec((groups, step, rows, lanes), lambda i: (0, i, 0, 0))] * 2
        + [whole(table)],
        out_specs=pl.BlockSpec((near, 2, step, rows_out, lanes), lambda i: (0, 0, i, 0, 0)),
        out_shape=jax.ShapeDtypeStruct((near, 2, channels, rows_out, lanes), F32),
        deps=deps,
        name="modes_to_cells",
    )


def mix_kernel(adjoint, groups, *refs):
    spec_refs, weight_ref, out_refs = refs[: CHUNKS * groups], refs[CHUNKS * groups], refs[-groups:]
    per_chunk = spec_refs[0].shape[0]
    rows = out_refs[0].shape[1] // 2
    for o in range(out_refs[0].shape[0]):
        real = [None] * groups
        imag = [None] * groups
        for i in range(CHUNKS * per_chunk):
            at = (o, i) if adjoint else (i, o)
            wr, wi = weight_ref[0, at[0], at[1]], weight_ref[1, at[0], at[1]]
            for s in range(groups):
                spec_ref = spec_refs[(i // per_chunk) * groups + s]
                sr = spec_ref[i % per_chunk, :rows]
                si = spec_ref[i % per_chunk, rows:]
                if adjoint:
                    re, im = wr * sr + wi * si, wr * si - wi * sr
                else:
                    re, im = wr * sr - wi * si, wr * si + wi * sr
                real[s] = re if i == 0 else real[s] + re
                imag[s] = im if i == 0 else imag[s] + im
        for s in range(groups):
            out_refs[s][o, :rows] = real[s]
            out_refs[s][o, rows:] = imag[s]


def mix(order, spectra, weight, q, adjoint):
    groups = len(spectra[0])
    per_chunk, rows, lanes = spectra[0][0].shape
    channels = weight.shape[1]
    step = 4
    if adjoint:
        block = (2, step, channels, rows // 2, lanes)
        place = lambda i: (0, q * (per_chunk // step) + i, 0, 0, 0)
    else:
        block = (2, channels, step, rows // 2, lanes)
        place = lambda i: (0, 0, q * (per_chunk // step) + i, 0, 0)
    flat = [piece for chunk in spectra for piece in chunk]
    return order.call(
        partial(mix_kernel, adjoint, groups),
        [*flat, weight],
        grid=(per_chunk // step,),
        in_specs=[whole(s) for s in flat] + [pl.BlockSpec(block, place)],
        out_specs=[pl.BlockSpec((step, rows, lanes), lambda i: (i, 0, 0))] * groups,
        out_shape=[jax.ShapeDtypeStruct((per_chunk, rows, lanes), F32)] * groups,
        name="mix_back" if adjoint else "mix",
    )


def weight_kernel(groups, *refs):
    grad_refs, spec_refs, out_ref = refs[: CHUNKS * groups], refs[CHUNKS * groups : -1], refs[-1]
    per_chunk = grad_refs[0].shape[0]
    rows = grad_refs[0].shape[1] // 2
    for i in range(out_ref.shape[1]):
        sr = [spec_refs[s][i, :rows] for s in range(groups)]
        si = [spec_refs[s][i, rows:] for s in range(groups)]
        for o in range(out_ref.shape[2]):
            real = imag = None
            for s in range(groups):
                grad_ref = grad_refs[(o // per_chunk) * groups + s]
                gr = grad_ref[o % per_chunk, :rows]
                gi = grad_ref[o % per_chunk, rows:]
                re, im = gr * sr[s] + gi * si[s], gi * sr[s] - gr * si[s]
                real = re if s == 0 else real + re
                imag = im if s == 0 else imag + im
            out_ref[0, i, o] = real
            out_ref[1, i, o] = imag


def weight_gradient(order, gradients, spectra, q, buffer, deps=()):
    groups = len(spectra)
    per_chunk, rows, lanes = spectra[0].shape
    channels = per_chunk * CHUNKS
    step = 2
    flat = [piece for chunk in gradients for piece in chunk]
    operands = flat + list(spectra)
    specs = [whole(g) for g in flat] + [
        pl.BlockSpec((step, rows, lanes), lambda i: (i, 0, 0)) for _ in spectra
    ]
    aliases = {}
    kernel = partial(weight_kernel, groups)
    if buffer is not None:
        aliases = {len(operands): 0}
        operands = operands + [buffer]
        specs = specs + [pl.BlockSpec(memory_space=pl.ANY)]
        kernel = lambda *refs: weight_kernel(groups, *refs[:-2], refs[-1])
    return order.call(
        kernel,
        [*operands],
        grid=(per_chunk // step,),
        in_specs=specs,
        out_specs=pl.BlockSpec(
            (2, step, channels, rows // 2, lanes),
            lambda i: (0, q * (per_chunk // step) + i, 0, 0, 0),
        ),
        out_shape=jax.ShapeDtypeStruct((2, channels, channels, rows // 2, lanes), F32),
        aliases=aliases,
        deps=deps,
        name="weight_gradient",
    )


def cut_lanes(modes, slabs):
    parts = slabs // HI
    if parts == 1:
        return modes
    _, channels, rows, lanes = modes.shape
    cut = modes.reshape(HI, channels, rows, parts, lanes // parts)
    return cut.transpose(0, 3, 1, 2, 4).reshape(slabs, channels, rows, lanes // parts)


def join_lanes(modes, slabs):
    parts = slabs // HI
    if parts == 1:
        return modes
    _, channels, rows, lanes = modes.shape
    cut = modes.reshape(HI, parts, channels, rows, lanes)
    return cut.transpose(0, 2, 3, 1, 4).reshape(HI, channels, rows, lanes * parts)


def shards(groups, slabs, fields, upstream, spectral_weight, point_weight, point_bias):
    near = slabs // 2
    half = lax.axis_index("mp") // near
    group = lax.axis_index("dp")

    def pick(tables, index):
        return lax.dynamic_index_in_dim(jnp.asarray(np.stack(tables)), index, 0, False)

    both = [(h, g) for h in range(2) for g in range(groups)]
    tx = pick([x_forward(groups, slabs, h, g) for h, g in both], half * groups + group)
    txi = pick([x_inverse(groups, slabs, h, g) for h, g in both], half * groups + group)
    ty = pick([y_forward(slabs, h) for h in range(2)], half)
    tyi = pick([y_inverse(slabs, h) for h in range(2)], half)
    tz, tz_scaled = jnp.asarray(z_forward(False)), jnp.asarray(z_forward(True))
    tzi, tzi_scaled = jnp.asarray(z_inverse(False)), jnp.asarray(z_inverse(True))
    halves = [[h * near + d for d in range(near)] for h in range(2)]
    across = [(j, j ^ near) for j in range(slabs)]

    def swap_near(data):
        return lax.all_to_all(
            data, "mp", split_axis=0, concat_axis=0, axis_index_groups=halves, tiled=True
        )

    def swap_groups(pieces):
        return [pieces[0]] + [
            lax.ppermute(pieces[k], "dp", [(j, j ^ k) for j in range(groups)])
            for k in range(1, groups)
        ]

    def near_blocks(planes):
        cut = cut_lanes(planes, slabs)
        return swap_near(cut.reshape((near, 2) + cut.shape[1:]))

    point = point_tables(point_weight, point_bias)
    point_back = point_tables(point_weight.T, jnp.zeros_like(point_bias))
    order = Order()
    state = {}

    def forward(q):
        planes = forward_planes(order, fields, q, ty, tz)
        state["near", q] = near_blocks(planes)

    def send(q):
        state["other", q] = lax.ppermute(line_send(order, state["near", q], tx), "mp", across)

    def keep(q):
        pieces = line_keep(order, state["near", q], state["other", q], tx, groups)
        state["spectrum", q] = swap_groups(pieces)

    def mixed(q, spectra, adjoint):
        own = jnp.stack(swap_groups(mix(order, spectra, spectral_weight, q, adjoint)))
        state["own", q] = own, lax.ppermute(own, "mp", across)

    def back(q, *deps):
        cells = swap_near(line_back(order, *state["own", q], txi, near, deps))
        state["planes", q] = join_lanes(cells.reshape((slabs,) + cells.shape[2:]), slabs)

    def channels(source, tables, key, q, *deps):
        state[key] = point_map(order, source, tables, q, state.get(key), deps)

    def middle(q):
        state["point"], planes = middle_planes(
            order, state["planes", q], state["point"], upstream, q, tzi_scaled, tyi, ty, tz_scaled
        )
        state["near", q] = near_blocks(planes)

    def weights(q, *deps):
        state["weights"] = weight_gradient(
            order, gradients, spectra[q], q, state.get("weights"), deps
        )

    def final(q):
        state["result"] = final_planes(order, state["planes", q], state["result"], q, tzi, tyi)

    map_fields = partial(channels, fields, point, "point")
    forward(0)
    map_fields(0)
    forward(1)
    send(0)
    map_fields(1)
    map_fields(2)
    send(1)
    keep(0)
    map_fields(3)
    keep(1)
    spectra = [state["spectrum", q] for q in range(CHUNKS)]
    mixed(0, spectra, False)
    mixed(1, spectra, False)
    back(0, state["own", 1][0])
    back(1)
    middle(0)
    middle(1)
    map_back = partial(channels, state["point"], point_back, "result")
    send(0)
    map_back(0)
    map_back(1)
    send(1)
    keep(0)
    map_back(2)
    map_back(3)
    keep(1)
    gradients = [state["spectrum", q] for q in range(CHUNKS)]
    mixed(0, gradients, True)
    mixed(1, gradients, True)
    weights(0, state["own", 0][0], state["own", 1][0])
    back(0)
    back(1)
    final(0)
    weights(1)
    final(1)
    return state["result"], state["weights"]


def solution(mesh):
    placed = (
        P("dp", None, "mp", None, None),
        P("dp", None, "mp", None, None),
        P(None, None, None, "dp", "mp"),
        P(),
        P(),
    )
    return jax.shard_map(
        partial(shards, mesh.shape["dp"], mesh.shape["mp"]),
        mesh=mesh,
        in_specs=placed,
        out_specs=(P("dp", None, "mp", None, None), P(None, None, None, "dp", "mp")),
        check_vma=False,
    )
```
